32 devices in a mesh: segment: 4 (over x, core), tensor: 8 (over z, y).
Axes of the slice: x: 2, y: 2, z: 4, core: 2. Of those that a mesh axis runs over, the one named last changes fastest.
Arguments:
- embeds: bfloat16 [2, 16, 6144], P(None, None, 'tensor'), may hold values from -6 to 6
- norm_gains: float32 [4, 2, 6144], P('segment'), may hold values from 0.5 to 2
- w_qkv: bfloat16 [4, 6144, 3, 8, 128], P('segment', None, None, 'tensor'), may hold values from -0.078125 to 0.078125
- w_out: bfloat16 [4, 8, 128, 6144], P('segment', 'tensor'), may hold values from -0.1875 to 0.1875
- w_up: bfloat16 [4, 6144, 1024], P('segment', None, 'tensor'), may hold values from -0.078125 to 0.078125
- w_down: bfloat16 [4, 1024, 6144], P('segment', 'tensor'), may hold values from -0.1875 to 0.1875
- cache: bfloat16 [4, 2, 16, 8, 64, 128], P('segment', None, None, 'tensor')
- lengths: int32 [16], replicated, may hold values from 1 to 64, as said below
- active_heads: int32 [4, 2, 2, 8], P('segment'), may hold values from 0 to 7, as said below
- active_blocks: int32 [4, 2, 2, 8], P('segment'), may hold values from 0 to 7, as said below
- active_counts: int32 [4, 2, 2, 2], P('segment'), may hold values from 1 to 8, as said below
Outputs:
- states: bfloat16 [4, 2, 16, 6144], P('segment', None, None, 'tensor')
The draws below stay inside these ranges and needn't reach their ends.
Inputs may be any that keep to these rules, and one draw needn't show every extreme that they name: `active_heads`: the first active_counts[...,0] entries of a list are distinct heads, the rest are 0. `active_blocks`: the first active_counts[...,1] entries of a list are distinct blocks, the rest are 0. `active_counts`: every list is full for the first micro-batch of the first step. `lengths`: some sequence has all 64 positions live.
All inputs are finite; a program needn't handle non-finite values.
Results may differ from the reference program's by a relative error of at most 0.024.
Values may be sent and summed in bfloat16 or wider, within the bound.
A program may use at most 64 MiB of HBM per device.

```python
import math
import jax
import jax.numpy as jnp
from jax import lax

D = 6144
HD = 128
BLOCK = 128
MB_SEQS = 8
MICRO = 2
STEPS = 2
CACHE = 64
LAYERS = 4
HEADS = 8
BLOCKS = 8
FF = 1024
SEQS = 16


def make_lists(key, salt, number):
    key = jax.random.fold_in(key, salt)
    first, second = jax.random.split(key)
    counts = jax.random.randint(first, (LAYERS, STEPS, MICRO), 1, number + 1)
    counts = counts.at[:, 0, 0].set(number)
    scores = jax.random.randint(second, (LAYERS, STEPS, MICRO, number), 0, 1048576) * number + jnp.arange(number)
    order = jnp.argsort(scores, axis=-1).astype(jnp.int32)
    listed = jnp.where(jnp.arange(number) < counts[..., None], order, 0)
    return (listed.astype(jnp.int32), counts.astype(jnp.int32))


def draw_active_heads(key, part):
    return make_lists(key, 11, HEADS)[0]


def draw_active_blocks(key, part):
    return make_lists(key, 13, BLOCKS)[0]


def draw_active_counts(key, part):
    head_counts = make_lists(key, 11, HEADS)[1]
    block_counts = make_lists(key, 13, BLOCKS)[1]
    return jnp.stack([head_counts, block_counts], -1).astype(jnp.int32)


def draw_lengths(key, part):
    key = jax.random.fold_in(key, 3)
    first, second = jax.random.split(key)
    sizes = jax.random.randint(first, (SEQS,), 1, CACHE + 1)
    where_full = jax.random.randint(second, (), 0, SEQS)
    return sizes.at[where_full].set(CACHE).astype(jnp.int32)


def draw_cache(key, part):
    key = jax.random.fold_in(key, 5)
    first = jax.random.fold_in(key, 0)
    values = jax.random.normal(first, (LAYERS, 2, SEQS, HEADS, CACHE, HD), jnp.float32)
    return values.astype(jnp.bfloat16)


def block_levels(key, shape, cuts, least, high):
    def one(position, shards_of):
        heights = jax.random.uniform(jax.random.fold_in(jax.random.fold_in(key, 6), position), (shards_of,), jnp.float32, least / len(cuts), high / len(cuts))
        return jnp.repeat(jnp.exp(heights), shape[position] // shards_of).reshape((-1,) + (1,) * (len(shape) - position - 1))

    factor_of = one(*cuts[0])
    for cut in cuts[1:]:
        factor_of = factor_of * one(*cut)
    return factor_of


def scatter_about(own_key, extent, width, bound, cuts=(), dtype=jnp.bfloat16):
    entries = width * jax.random.normal(own_key, extent, jnp.float32)
    if cuts:
        entries = entries * block_levels(own_key, extent, cuts, -0.22, 0.18)
    return jnp.clip(entries, -bound, bound).astype(dtype)


def setup_inputs(seed: int = 0) -> dict:
    splits = jax.random.split(jax.random.key(seed), 12)
    return {
        "embeds": scatter_about(splits[0], (STEPS, SEQS, D), 1.0, 6.0, ((2, 8),)),
        "norm_gains": jnp.clip(jnp.exp(math.log(2.0) - 1.3862944 * jax.random.uniform(splits[1], (LAYERS, 2, D), jnp.float32) ** block_levels(splits[1], (LAYERS, 2, D), ((0, 4),), -0.2, 0.2)), 0.5, 2.0),
        "w_qkv": scatter_about(splits[2], (LAYERS, D, 3, HEADS, HD), D ** -0.5, 0.078125, ((0, 4), (3, 8))),
        "w_out": scatter_about(splits[3], (LAYERS, HEADS, HD, D), (HEADS * HD) ** -0.5, 0.1875, ((0, 4), (1, 8))),
        "w_up": scatter_about(splits[4], (LAYERS, D, FF), D ** -0.5, 0.078125, ((0, 4), (2, 8))),
        "w_down": scatter_about(splits[5], (LAYERS, FF, D), FF ** -0.5, 0.1875, ((0, 4), (1, 8))),
        "cache": draw_cache(jax.random.fold_in(splits[11], 71), 0),
        "lengths": draw_lengths(jax.random.fold_in(splits[11], 71), 0),
        "active_heads": draw_active_heads(jax.random.fold_in(splits[11], 71), 0),
        "active_blocks": draw_active_blocks(jax.random.fold_in(splits[11], 71), 0),
        "active_counts": draw_active_counts(jax.random.fold_in(splits[11], 71), 0),
    }


EPS = 1e-05

def normed(x, gain):
    values = x.astype(jnp.float32)
    mean = lax.optimization_barrier(jnp.mean(values, -1, keepdims=True))
    var = lax.optimization_barrier(jnp.mean((values - mean) ** 2, -1, keepdims=True))
    return ((values - mean) * lax.rsqrt(var + EPS) * gain).astype(jnp.bfloat16)

def member_mask(ids, counts, number):
    slots = jnp.arange(ids.shape[-1]) < counts[..., None]
    hits = (ids[..., :, None] == jnp.arange(number)) & slots[..., :, None]
    return jnp.any(hits, axis=-2).astype(jnp.float32)

def reference(embeds, norm_gains, w_qkv, w_out, w_up, w_down, cache, lengths, active_heads, active_blocks, active_counts):
    heads_on = jnp.repeat(member_mask(active_heads, active_counts[..., 0], HEADS), MB_SEQS, axis=2)
    blocks_on = jnp.repeat(member_mask(active_blocks, active_counts[..., 1], BLOCKS), MB_SEQS, axis=2)
    cache_live = jnp.arange(CACHE)[None, :] < lengths[:, None]
    scale = HD ** (-0.5)
    fresh_all = jnp.zeros((LAYERS, STEPS, 2, SEQS, HEADS, HD), jnp.bfloat16)
    outputs = []
    for step in range(STEPS):

        def layer(x, inputs):
            gains, proj, out_proj, up_w, down_w, stored, head_mask, block_mask, fresh = inputs
            h = normed(x, gains[0])
            qkv = jnp.einsum('sd,dchk->schk', h.astype(jnp.float32), proj.astype(jnp.float32)).astype(jnp.bfloat16)
            fresh = fresh.at[step, 0].set(qkv[:, 1]).at[step, 1].set(qkv[:, 2])
            query = qkv[:, 0].astype(jnp.float32)
            old = jnp.einsum('shk,shpk->shp', query, stored[0].astype(jnp.float32)) * scale
            old = jnp.where(cache_live[:, None, :], old, -jnp.inf)
            new = jnp.einsum('shk,ushk->shu', query, fresh[:, 0].astype(jnp.float32)) * scale
            new = jnp.where(jnp.arange(STEPS)[None, None, :] <= step, new, -jnp.inf)
            probs = jax.nn.softmax(jnp.concatenate([old, new], -1), -1).astype(jnp.bfloat16)
            values = jnp.concatenate([stored[1], jnp.transpose(fresh[:, 1], (1, 2, 0, 3))], 2)
            mixed = jnp.einsum('shp,shpk->shk', probs.astype(jnp.float32), values.astype(jnp.float32)).astype(jnp.bfloat16)
            attn = jnp.einsum('shk,hkd->sd', mixed.astype(jnp.float32) * head_mask[:, :, None], out_proj.astype(jnp.float32))
            first = (x.astype(jnp.float32) + attn).astype(jnp.bfloat16)
            second_in = normed(first, gains[1])
            upper = jnp.dot(second_in, up_w, preferred_element_type=jnp.float32)
            active = jax.nn.relu(upper).astype(jnp.bfloat16) * jnp.repeat(block_mask, BLOCK, axis=1).astype(jnp.bfloat16)
            lower = jnp.dot(active, down_w, preferred_element_type=jnp.float32)
            result = (first.astype(jnp.float32) + lower).astype(jnp.bfloat16)
            return (result, (result, fresh))
        inputs = (norm_gains, w_qkv, w_out, w_up, w_down, cache, heads_on[:, step], blocks_on[:, step], fresh_all)
        last, (layer_states, fresh_all) = lax.scan(layer, embeds[step], inputs)
        outputs.append(layer_states)
    return jnp.stack(outputs, axis=1)
```

```python
import functools

import jax
import jax.numpy as jnp
from jax import lax
from jax.experimental import pallas as pl
from jax.experimental.pallas import tpu as pltpu
from jax.sharding import PartitionSpec as P

EPS = 1e-05
GROUPS = 1
MESH_ID = pl.DeviceIdType.MESH


def partner_order(members):
    return sorted(range(1, members), key=lambda k: (-min(k, members - k), k))


def relay_kernel(
    sizes,
    embeds,
    gains,
    w_qkv,
    w_out,
    w_up,
    w_down,
    cache,
    lengths,
    heads,
    blocks,
    counts,
    out,
    qkv_w,
    out_w,
    up_w,
    down_w,
    kv,
    load_sem,
    x_in,
    first_in,
    part_out,
    part_in,
    x_recv,
    first_recv,
    part_recv,
    x_send,
    first_send,
    part_send,
    next_send,
    first_own,
    next_own,
):
    segments, members, steps, seqs, micro, groups = sizes
    piece = embeds.shape[1]
    width = piece * members
    rows = steps * seqs // groups
    steps_in = steps // groups
    head_dim = w_qkv.shape[2]
    positions = cache.shape[1] // seqs
    group = seqs // micro
    segment = lax.axis_index("segment")
    rank = lax.axis_index("tensor")
    order = partner_order(members)

    def other(k):
        return lax.rem(rank + k, members)

    loads = [
        pltpu.make_async_copy(
            w_qkv.at[j], qkv_w.at[:, pl.ds(j * head_dim, head_dim)], load_sem.at[j]
        )
        for j in range(3)
    ]
    loads.append(pltpu.make_async_copy(cache, kv, load_sem.at[3]))
    loads.append(pltpu.make_async_copy(w_out, out_w, load_sem.at[4]))
    loads.append(pltpu.make_async_copy(w_up, up_w, load_sem.at[5]))
    loads.append(pltpu.make_async_copy(w_down, down_w, load_sem.at[6]))
    for load in loads:
        load.start()

    barrier = pltpu.get_barrier_semaphore()
    for k in range(1, members):
        pl.semaphore_signal(barrier, inc=1, device_id=(segment, other(k)), device_id_type=MESH_ID)

    @pl.when(segment > 0)
    def _():
        for k in range(members):
            pl.semaphore_signal(
                barrier, inc=1, device_id=(segment - 1, other(k)), device_id_type=MESH_ID
            )

    @pl.when(segment < segments - 1)
    def _():
        for k in range(members):
            pl.semaphore_signal(
                barrier, inc=1, device_id=(segment + 1, other(k)), device_id_type=MESH_ID
            )

    inner = (segment > 0) & (segment < segments - 1)

    @pl.when(inner)
    def _():
        pl.semaphore_wait(barrier, 3 * members - 1)

    @pl.when(jnp.logical_not(inner))
    def _():
        pl.semaphore_wait(barrier, 2 * members - 1)

    def send(src, dst, send_sem, recv_sem, target):
        return pltpu.make_async_remote_copy(
            src_ref=src,
            dst_ref=dst,
            send_sem=send_sem,
            recv_sem=recv_sem,
            device_id=target,
            device_id_type=MESH_ID,
        )

    def arrival(buffer, sem):
        return send(buffer, buffer, sem, sem, (segment, other(1)))

    def x_copy(g, k):
        return send(
            embeds.at[pl.ds(g * rows, rows)],
            x_in.at[g, rank],
            x_send.at[g, k],
            x_recv.at[g, rank],
            (segment, other(k)),
        )

    @pl.when(segment == 0)
    def _():
        for g in range(groups):
            for k in order:
                x_copy(g, k).start()
            x_in[g, rank] = embeds[g * rows : (g + 1) * rows]

    row_ids = lax.broadcasted_iota(jnp.int32, (steps * seqs, 1), 0)
    row_seq = lax.rem(row_ids, seqs)
    row_len = jnp.zeros((steps * seqs, 1), jnp.int32)
    for s in range(seqs):
        row_len = jnp.where(row_seq == s, lengths[s], row_len)

    def live_rows(lists, which):
        live = jnp.zeros((steps * seqs, 1), jnp.int32)
        for t in range(steps):
            for m in range(micro):
                hit = jnp.int32(0)
                for j in range(lists.shape[2]):
                    same = (lists[t, m, j] == rank) & (j < counts[t, m, which])
                    hit = hit + same.astype(jnp.int32)
                start = t * seqs + m * group
                inside = (row_ids >= start) & (row_ids < start + group)
                live = jnp.where(inside, hit, live)
        return live > 0

    head_live = live_rows(heads, 0)
    block_live = live_rows(blocks, 1)

    def span(p):
        return slice(p * piece, (p + 1) * piece)

    def normalized(buffer, g, which):
        total = jnp.zeros((rows, 1), jnp.float32)
        for p in range(members):
            total = total + jnp.sum(buffer[g, p].astype(jnp.float32), -1, keepdims=True)
        mean = total / width
        square = jnp.zeros((rows, 1), jnp.float32)
        for p in range(members):
            off = buffer[g, p].astype(jnp.float32) - mean
            square = square + jnp.sum(off * off, -1, keepdims=True)
        inverse = lax.rsqrt(square / width + EPS)
        for p in range(members):
            off = buffer[g, p].astype(jnp.float32) - mean
            yield p, (off * inverse * gains[which : which + 1, span(p)]).astype(jnp.bfloat16)

    def columns(p):
        return pl.ds(pl.multiple_of(p * piece, piece), piece)

    def part_copy(phase, g, k):
        return send(
            part_out.at[phase, g, k],
            part_in.at[phase, g, rank],
            part_send.at[phase, g, k],
            part_recv.at[phase, g, rank],
            (segment, other(k)),
        )

    def scatter(values, weight, phase, g):
        for k in order:
            part = jnp.dot(values, weight[:, columns(other(k))], preferred_element_type=jnp.float32)
            part_out[phase, g, k] = part.astype(jnp.bfloat16)
            part_copy(phase, g, k).start()
        return jnp.dot(values, weight[:, columns(rank)], preferred_element_type=jnp.float32)

    def gather_sum(total, phase, g):
        for k in reversed(order):
            p = other(k)
            arrival(part_in.at[phase, g, p], part_recv.at[phase, g, p]).wait_recv()
            total = total + part_in[phase, g, p].astype(jnp.float32)
        return total

    def first_copy(g, k):
        return send(
            first_own.at[g],
            first_in.at[g, rank],
            first_send.at[g, k],
            first_recv.at[g, rank],
            (segment, other(k)),
        )

    def next_copy(g, k):
        return send(
            next_own.at[g],
            x_in.at[g, rank],
            next_send.at[g, k],
            x_recv.at[g, rank],
            (segment + 1, other(k)),
        )

    fresh_keys, fresh_values = [], []

    def attend(g):
        qkv = jnp.zeros((rows, 3 * head_dim), jnp.float32)
        for p, h in normalized(x_in, g, 0):
            qkv = qkv + jnp.dot(h, qkv_w[span(p), :], preferred_element_type=jnp.float32)
        qkv = qkv.astype(jnp.bfloat16)
        query = qkv[:, :head_dim]
        fresh_keys.append(qkv[:, head_dim : 2 * head_dim])
        fresh_values.append(qkv[:, 2 * head_dim :])
        scale = head_dim ** (-0.5)
        contract = (((1,), (1,)), ((), ()))
        mine = slice(g * rows, (g + 1) * rows)
        old = lax.dot_general(query, kv[0], contract, preferred_element_type=jnp.float32) * scale
        where = lax.broadcasted_iota(jnp.int32, old.shape, 1)
        start = row_seq[mine] * positions
        live = (where >= start) & (where < start + row_len[mine])
        old = jnp.where(live, old, -jnp.inf)
        top = jnp.max(old, -1, keepdims=True)
        fresh = []
        for u, keys in enumerate(fresh_keys):
            new = lax.dot_general(query, keys, contract, preferred_element_type=jnp.float32) * scale
            seen = lax.broadcasted_iota(jnp.int32, new.shape, 1) + u * rows
            seen_ok = (lax.rem(seen, seqs) == row_seq[mine]) & (seen <= row_ids[mine])
            new = jnp.where(seen_ok, new, -jnp.inf)
            top = jnp.maximum(top, jnp.max(new, -1, keepdims=True))
            fresh.append(new)
        old = jnp.exp(old - top)
        norm = jnp.sum(old, -1, keepdims=True)
        fresh = [jnp.exp(new - top) for new in fresh]
        for new in fresh:
            norm = norm + jnp.sum(new, -1, keepdims=True)
        mixed = jnp.dot(
            (old / norm).astype(jnp.bfloat16), kv[1], preferred_element_type=jnp.float32
        )
        for new, values in zip(fresh, fresh_values):
            mixed = mixed + jnp.dot(
                (new / norm).astype(jnp.bfloat16), values, preferred_element_type=jnp.float32
            )
        return jnp.where(head_live[mine], mixed, 0.0).astype(jnp.bfloat16)

    def feed(g):
        upper = jnp.zeros((rows, up_w.shape[1]), jnp.float32)
        for p, h in normalized(first_in, g, 1):
            upper = upper + jnp.dot(h, up_w[span(p), :], preferred_element_type=jnp.float32)
        mine = slice(g * rows, (g + 1) * rows)
        return jnp.where(block_live[mine], jnp.maximum(upper, 0.0), 0.0).astype(jnp.bfloat16)

    sums = [None] * groups
    for g in range(groups):
        for k in order:
            p = other(k)
            arrival(x_in.at[g, p], x_recv.at[g, p]).wait_recv()

        @pl.when(segment > 0)
        def _():
            arrival(x_in.at[g, rank], x_recv.at[g, rank]).wait_recv()

        if g == 0:
            for load in loads[:4]:
                load.wait()
        mixed = attend(g)
        if g == 0:
            loads[4].wait()
        sums[g] = scatter(mixed, out_w, 0, g)
    for g in range(groups):
        attn = gather_sum(sums[g], 0, g)
        first = (x_in[g, rank].astype(jnp.float32) + attn).astype(jnp.bfloat16)
        first_own[g] = first
        for k in order:
            first_copy(g, k).start()
        first_in[g, rank] = first
    for load in loads[5:]:
        load.wait()
    for g in range(groups):
        for k in order:
            p = other(k)
            arrival(first_in.at[g, p], first_recv.at[g, p]).wait_recv()
        sums[g] = scatter(feed(g), down_w, 1, g)
    for g in range(groups):
        lower = gather_sum(sums[g], 1, g)
        result = (first_own[g].astype(jnp.float32) + lower).astype(jnp.bfloat16)
        next_own[g] = result

        @pl.when(segment < segments - 1)
        def _():
            for k in [*order, 0]:
                next_copy(g, k).start()

        out[g * rows : (g + 1) * rows] = result

    for g in range(groups):

        @pl.when(segment == 0)
        def _():
            for k in order:
                x_copy(g, k).wait_send()

        for k in order:
            part_copy(0, g, k).wait_send()
            first_copy(g, k).wait_send()
            part_copy(1, g, k).wait_send()

        @pl.when(segment < segments - 1)
        def _():
            for k in [*order, 0]:
                next_copy(g, k).wait_send()


def body(
    embeds,
    norm_gains,
    w_qkv,
    w_out,
    w_up,
    w_down,
    cache,
    lengths,
    active_heads,
    active_blocks,
    active_counts,
):
    segments = lax.axis_size("segment")
    members = lax.axis_size("tensor")
    steps, seqs, piece = embeds.shape
    micro = active_heads.shape[2]
    width = piece * members
    head_dim = w_qkv.shape[-1]
    block = w_up.shape[2]
    positions = cache.shape[4]
    groups = GROUPS
    rows = steps * seqs // groups
    bf16 = jnp.bfloat16
    vmem = pl.BlockSpec(memory_space=pltpu.VMEM)
    smem = pl.BlockSpec(memory_space=pltpu.SMEM)
    hbm = pl.BlockSpec(memory_space=pl.ANY)
    dma = pltpu.SemaphoreType.DMA
    sizes = (segments, members, steps, seqs, micro, groups)
    flops = 2 * steps * seqs * width * (4 * head_dim + 2 * block)
    states = pl.pallas_call(
        functools.partial(relay_kernel, sizes),
        out_shape=jax.ShapeDtypeStruct((steps * seqs, piece), bf16),
        in_specs=[vmem, vmem, hbm, hbm, hbm, hbm, hbm, smem, smem, smem, smem],
        out_specs=vmem,
        scratch_shapes=[
            pltpu.VMEM((width, 3 * head_dim), bf16),
            pltpu.VMEM((head_dim, width), bf16),
            pltpu.VMEM((width, block), bf16),
            pltpu.VMEM((block, width), bf16),
            pltpu.VMEM((2, seqs * positions, head_dim), bf16),
            dma((7,)),
            pltpu.VMEM((groups, members, rows, piece), bf16),
            pltpu.VMEM((groups, members, rows, piece), bf16),
            pltpu.VMEM((2, groups, members, rows, piece), bf16),
            pltpu.VMEM((2, groups, members, rows, piece), bf16),
            dma((groups, members)),
            dma((groups, members)),
            dma((2, groups, members)),
            dma((groups, members)),
            dma((groups, members)),
            dma((2, groups, members)),
            dma((groups, members)),
            pltpu.VMEM((groups, rows, piece), bf16),
            pltpu.VMEM((groups, rows, piece), bf16),
        ],
        compiler_params=pltpu.CompilerParams(
            collective_id=0, has_side_effects=True, vmem_limit_bytes=48 * 1024 * 1024
        ),
        cost_estimate=pl.CostEstimate(
            flops=flops, bytes_accessed=2 * width * (4 * head_dim + 2 * block), transcendentals=0
        ),
    )(
        embeds.reshape(steps * seqs, piece),
        norm_gains[0],
        jnp.transpose(w_qkv, (0, 2, 3, 1, 4)).reshape(3, width, head_dim),
        w_out[0, 0],
        w_up[0],
        w_down[0],
        cache.reshape(2, seqs * positions, head_dim),
        lengths,
        active_heads[0],
        active_blocks[0],
        active_counts[0],
    )
    return states.reshape(1, steps, seqs, piece)


def solution(mesh):
    in_specs = (
        P(None, None, "tensor"),
        P("segment", None, None),
        P("segment", None, None, "tensor", None),
        P("segment", "tensor", None, None),
        P("segment", None, "tensor"),
        P("segment", "tensor", None),
        P("segment", None, None, "tensor", None, None),
        P(),
        P("segment", None, None, None),
        P("segment", None, None, None),
        P("segment", None, None, None),
    )
    out_specs = P("segment", None, None, "tensor")
    return jax.shard_map(body, mesh=mesh, in_specs=in_specs, out_specs=out_specs, check_vma=False)
```

```python
import functools

import jax
import jax.numpy as jnp
from jax import lax
from jax.experimental import pallas as pl
from jax.experimental.pallas import tpu as pltpu
from jax.sharding import PartitionSpec as P

EPS = 1e-05
GROUPS = 2
MESH_ID = pl.DeviceIdType.MESH


def partner_order(members):
    return sorted(range(1, members), key=lambda k: (-min(k, members - k), k))


def relay_kernel(
    sizes,
    embeds_at,
    gains_at,
    w_qkv,
    w_out,
    w_up,
    w_down,
    cache,
    lengths_at,
    heads_at,
    blocks_at,
    counts_at,
    out,
    embeds,
    gains,
    lengths,
    heads,
    blocks,
    counts,
    small_sem,
    qkv_w,
    out_w,
    up_w,
    down_w,
    kv,
    load_sem,
    x_in,
    first_in,
    part_out,
    part_in,
    x_recv,
    first_recv,
    part_recv,
    x_send,
    first_send,
    part_send,
    next_send,
    first_own,
    next_own,
):
    segments, members, steps, seqs, micro, groups = sizes
    piece = embeds.shape[1]
    width = piece * members
    rows = steps * seqs // groups
    steps_in = steps // groups
    head_dim = w_qkv.shape[2]
    positions = cache.shape[1] // seqs
    group = seqs // micro
    segment = lax.axis_index("segment")
    rank = lax.axis_index("tensor")
    order = partner_order(members)

    def other(k):
        return lax.rem(rank + k, members)

    small = [
        pltpu.make_async_copy(source, target, small_sem.at[i])
        for i, (source, target) in enumerate(
            [
                (embeds_at, embeds),
                (lengths_at, lengths),
                (heads_at, heads),
                (blocks_at, blocks),
                (counts_at, counts),
                (gains_at, gains),
            ]
        )
    ]
    for load in small:
        load.start()
    loads = [
        pltpu.make_async_copy(
            w_qkv.at[j], qkv_w.at[:, pl.ds(j * head_dim, head_dim)], load_sem.at[j]
        )
        for j in range(3)
    ]
    loads.append(pltpu.make_async_copy(cache, kv, load_sem.at[3]))
    loads.append(pltpu.make_async_copy(w_out, out_w, load_sem.at[4]))
    loads.append(pltpu.make_async_copy(w_up, up_w, load_sem.at[5]))
    loads.append(pltpu.make_async_copy(w_down, down_w, load_sem.at[6]))
    for load in loads:
        load.start()

    barrier = pltpu.get_barrier_semaphore()
    for k in range(1, members):
        pl.semaphore_signal(barrier, inc=1, device_id=(segment, other(k)), device_id_type=MESH_ID)

    @pl.when(segment > 0)
    def _():
        for k in range(members):
            pl.semaphore_signal(
                barrier, inc=1, device_id=(segment - 1, other(k)), device_id_type=MESH_ID
            )

    @pl.when(segment < segments - 1)
    def _():
        for k in range(members):
            pl.semaphore_signal(
                barrier, inc=1, device_id=(segment + 1, other(k)), device_id_type=MESH_ID
            )

    inner = (segment > 0) & (segment < segments - 1)

    @pl.when(inner)
    def _():
        pl.semaphore_wait(barrier, 3 * members - 1)

    @pl.when(jnp.logical_not(inner))
    def _():
        pl.semaphore_wait(barrier, 2 * members - 1)

    def send(src, dst, send_sem, recv_sem, target):
        return pltpu.make_async_remote_copy(
            src_ref=src,
            dst_ref=dst,
            send_sem=send_sem,
            recv_sem=recv_sem,
            device_id=target,
            device_id_type=MESH_ID,
        )

    def arrival(buffer, sem):
        return send(buffer, buffer, sem, sem, (segment, other(1)))

    def x_copy(g, k):
        return send(
            embeds.at[pl.ds(g * rows, rows)],
            x_in.at[g, rank],
            x_send.at[g, k],
            x_recv.at[g, rank],
            (segment, other(k)),
        )

    small[0].wait()

    @pl.when(segment == 0)
    def _():
        for g in range(groups):
            for k in order:
                x_copy(g, k).start()
            x_in[g, rank] = embeds[g * rows : (g + 1) * rows]

    for load in small[1:]:
        load.wait()
    row_ids = lax.broadcasted_iota(jnp.int32, (steps * seqs, 1), 0)
    row_seq = lax.rem(row_ids, seqs)
    row_len = jnp.zeros((steps * seqs, 1), jnp.int32)
    for s in range(seqs):
        row_len = jnp.where(row_seq == s, lengths[s], row_len)

    def live_rows(lists, which):
        live = jnp.zeros((steps * seqs, 1), jnp.int32)
        for t in range(steps):
            for m in range(micro):
                hit = jnp.int32(0)
                for j in range(lists.shape[2]):
                    same = (lists[t, m, j] == rank) & (j < counts[t, m, which])
                    hit = hit + same.astype(jnp.int32)
                start = t * seqs + m * group
                inside = (row_ids >= start) & (row_ids < start + group)
                live = jnp.where(inside, hit, live)
        return live > 0

    head_live = live_rows(heads, 0)
    block_live = live_rows(blocks, 1)

    def span(p):
        return slice(p * piece, (p + 1) * piece)

    def normalized(buffer, g, which):
        total = jnp.zeros((rows, 1), jnp.float32)
        for p in range(members):
            total = total + jnp.sum(buffer[g, p].astype(jnp.float32), -1, keepdims=True)
        mean = total / width
        square = jnp.zeros((rows, 1), jnp.float32)
        for p in range(members):
            off = buffer[g, p].astype(jnp.float32) - mean
            square = square + jnp.sum(off * off, -1, keepdims=True)
        inverse = lax.rsqrt(square / width + EPS)
        for p in range(members):
            off = buffer[g, p].astype(jnp.float32) - mean
            yield p, (off * inverse * gains[which : which + 1, span(p)]).astype(jnp.bfloat16)

    def columns(p):
        return pl.ds(pl.multiple_of(p * piece, piece), piece)

    def part_copy(phase, g, k):
        return send(
            part_out.at[phase, g, k],
            part_in.at[phase, g, rank],
            part_send.at[phase, g, k],
            part_recv.at[phase, g, rank],
            (segment, other(k)),
        )

    def scatter(values, weight, phase, g):
        for k in order:
            part = jnp.dot(values, weight[:, columns(other(k))], preferred_element_type=jnp.float32)
            part_out[phase, g, k] = part.astype(jnp.bfloat16)
            part_copy(phase, g, k).start()
        return jnp.dot(values, weight[:, columns(rank)], preferred_element_type=jnp.float32)

    def gather_sum(total, phase, g):
        for k in reversed(order):
            p = other(k)
            arrival(part_in.at[phase, g, p], part_recv.at[phase, g, p]).wait_recv()
            total = total + part_in[phase, g, p].astype(jnp.float32)
        return total

    def first_copy(g, k):
        return send(
            first_own.at[g],
            first_in.at[g, rank],
            first_send.at[g, k],
            first_recv.at[g, rank],
            (segment, other(k)),
        )

    def next_copy(g, k):
        return send(
            next_own.at[g],
            x_in.at[g, rank],
            next_send.at[g, k],
            x_recv.at[g, rank],
            (segment + 1, other(k)),
        )

    fresh_keys, fresh_values = [], []

    def attend(g):
        qkv = jnp.zeros((rows, 3 * head_dim), jnp.float32)
        for p, h in normalized(x_in, g, 0):
            qkv = qkv + jnp.dot(h, qkv_w[span(p), :], preferred_element_type=jnp.float32)
        qkv = qkv.astype(jnp.bfloat16)
        query = qkv[:, :head_dim]
        fresh_keys.append(qkv[:, head_dim : 2 * head_dim])
        fresh_values.append(qkv[:, 2 * head_dim :])
        scale = head_dim ** (-0.5)
        contract = (((1,), (1,)), ((), ()))
        mine = slice(g * rows, (g + 1) * rows)
        old = lax.dot_general(query, kv[0], contract, preferred_element_type=jnp.float32) * scale
        where = lax.broadcasted_iota(jnp.int32, old.shape, 1)
        start = row_seq[mine] * positions
        live = (where >= start) & (where < start + row_len[mine])
        old = jnp.where(live, old, -jnp.inf)
        top = jnp.max(old, -1, keepdims=True)
        fresh = []
        for u, keys in enumerate(fresh_keys):
            new = lax.dot_general(query, keys, contract, preferred_element_type=jnp.float32) * scale
            seen = lax.broadcasted_iota(jnp.int32, new.shape, 1) + u * rows
            seen_ok = (lax.rem(seen, seqs) == row_seq[mine]) & (seen <= row_ids[mine])
            new = jnp.where(seen_ok, new, -jnp.inf)
            top = jnp.maximum(top, jnp.max(new, -1, keepdims=True))
            fresh.append(new)
        old = jnp.exp(old - top)
        norm = jnp.sum(old, -1, keepdims=True)
        fresh = [jnp.exp(new - top) for new in fresh]
        for new in fresh:
            norm = norm + jnp.sum(new, -1, keepdims=True)
        mixed = jnp.dot(
            (old / norm).astype(jnp.bfloat16), kv[1], preferred_element_type=jnp.float32
        )
        for new, values in zip(fresh, fresh_values):
            mixed = mixed + jnp.dot(
                (new / norm).astype(jnp.bfloat16), values, preferred_element_type=jnp.float32
            )
        return jnp.where(head_live[mine], mixed, 0.0).astype(jnp.bfloat16)

    def feed(g):
        upper = jnp.zeros((rows, up_w.shape[1]), jnp.float32)
        for p, h in normalized(first_in, g, 1):
            upper = upper + jnp.dot(h, up_w[span(p), :], preferred_element_type=jnp.float32)
        mine = slice(g * rows, (g + 1) * rows)
        return jnp.where(block_live[mine], jnp.maximum(upper, 0.0), 0.0).astype(jnp.bfloat16)

    sums = [None] * groups
    for g in range(groups):
        for k in order:
            p = other(k)
            arrival(x_in.at[g, p], x_recv.at[g, p]).wait_recv()

        @pl.when(segment > 0)
        def _():
            arrival(x_in.at[g, rank], x_recv.at[g, rank]).wait_recv()

        if g == 0:
            for load in loads[:4]:
                load.wait()
        mixed = attend(g)
        if g == 0:
            loads[4].wait()
        sums[g] = scatter(mixed, out_w, 0, g)
    for g in range(groups):
        attn = gather_sum(sums[g], 0, g)
        first = (x_in[g, rank].astype(jnp.float32) + attn).astype(jnp.bfloat16)
        first_own[g] = first
        for k in order:
            first_copy(g, k).start()
        first_in[g, rank] = first
    for load in loads[5:]:
        load.wait()
    for g in range(groups):
        for k in order:
            p = other(k)
            arrival(first_in.at[g, p], first_recv.at[g, p]).wait_recv()
        sums[g] = scatter(feed(g), down_w, 1, g)
    for g in range(groups):
        lower = gather_sum(sums[g], 1, g)
        result = (first_own[g].astype(jnp.float32) + lower).astype(jnp.bfloat16)
        next_own[g] = result

        @pl.when(segment < segments - 1)
        def _():
            for k in [*order, 0]:
                next_copy(g, k).start()

        out[g * rows : (g + 1) * rows] = result

    for g in range(groups):

        @pl.when(segment == 0)
        def _():
            for k in order:
                x_copy(g, k).wait_send()

        for k in order:
            part_copy(0, g, k).wait_send()
            first_copy(g, k).wait_send()
            part_copy(1, g, k).wait_send()

        @pl.when(segment < segments - 1)
        def _():
            for k in [*order, 0]:
                next_copy(g, k).wait_send()


def body(
    embeds,
    norm_gains,
    w_qkv,
    w_out,
    w_up,
    w_down,
    cache,
    lengths,
    active_heads,
    active_blocks,
    active_counts,
):
    segments = lax.axis_size("segment")
    members = lax.axis_size("tensor")
    steps, seqs, piece = embeds.shape
    micro = active_heads.shape[2]
    width = piece * members
    head_dim = w_qkv.shape[-1]
    block = w_up.shape[2]
    positions = cache.shape[4]
    groups = GROUPS
    rows = steps * seqs // groups
    bf16 = jnp.bfloat16
    vmem = pl.BlockSpec(memory_space=pltpu.VMEM)
    hbm = pl.BlockSpec(memory_space=pl.ANY)
    dma = pltpu.SemaphoreType.DMA
    sizes = (segments, members, steps, seqs, micro, groups)
    flops = 2 * steps * seqs * width * (4 * head_dim + 2 * block)
    states = pl.pallas_call(
        functools.partial(relay_kernel, sizes),
        out_shape=jax.ShapeDtypeStruct((steps * seqs, piece), bf16),
        in_specs=[hbm] * 11,
        out_specs=vmem,
        scratch_shapes=[
            pltpu.VMEM((steps * seqs, piece), bf16),
            pltpu.VMEM(norm_gains.shape[1:], jnp.float32),
            pltpu.SMEM(lengths.shape, jnp.int32),
            pltpu.SMEM(active_heads.shape[1:], jnp.int32),
            pltpu.SMEM(active_blocks.shape[1:], jnp.int32),
            pltpu.SMEM(active_counts.shape[1:], jnp.int32),
            dma((6,)),
            pltpu.VMEM((width, 3 * head_dim), bf16),
            pltpu.VMEM((head_dim, width), bf16),
            pltpu.VMEM((width, block), bf16),
            pltpu.VMEM((block, width), bf16),
            pltpu.VMEM((2, seqs * positions, head_dim), bf16),
            dma((7,)),
            pltpu.VMEM((groups, members, rows, piece), bf16),
            pltpu.VMEM((groups, members, rows, piece), bf16),
            pltpu.VMEM((2, groups, members, rows, piece), bf16),
            pltpu.VMEM((2, groups, members, rows, piece), bf16),
            dma((groups, members)),
            dma((groups, members)),
            dma((2, groups, members)),
            dma((groups, members)),
            dma((groups, members)),
            dma((2, groups, members)),
            dma((groups, members)),
            pltpu.VMEM((groups, rows, piece), bf16),
            pltpu.VMEM((groups, rows, piece), bf16),
        ],
        compiler_params=pltpu.CompilerParams(
            collective_id=0, has_side_effects=True, vmem_limit_bytes=56 * 1024 * 1024
        ),
        cost_estimate=pl.CostEstimate(
            flops=flops, bytes_accessed=2 * width * (4 * head_dim + 2 * block), transcendentals=0
        ),
    )(
        embeds.reshape(steps * seqs, piece),
        norm_gains[0],
        jnp.transpose(w_qkv, (0, 2, 3, 1, 4)).reshape(3, width, head_dim),
        w_out[0, 0],
        w_up[0],
        w_down[0],
        cache.reshape(2, seqs * positions, head_dim),
        lengths,
        active_heads[0],
        active_blocks[0],
        active_counts[0],
    )
    return states.reshape(1, steps, seqs, piece)


def solution(mesh):
    in_specs = (
        P(None, None, "tensor"),
        P("segment", None, None),
        P("segment", None, None, "tensor", None),
        P("segment", "tensor", None, None),
        P("segment", None, "tensor"),
        P("segment", "tensor", None),
        P("segment", None, None, "tensor", None, None),
        P(),
        P("segment", None, None, None),
        P("segment", None, None, None),
        P("segment", None, None, None),
    )
    out_specs = P("segment", None, None, "tensor")
    return jax.shard_map(body, mesh=mesh, in_specs=in_specs, out_specs=out_specs, check_vma=False)
```

```python
import functools

import jax
import jax.numpy as jnp
from jax import lax
from jax.experimental import pallas as pl
from jax.experimental.pallas import tpu as pltpu
from jax.sharding import PartitionSpec as P

EPS = 1e-05
GROUPS = 2
MESH_ID = pl.DeviceIdType.MESH


def partner_order(members):
    return list(range(1, members))


def relay_kernel(
    sizes,
    embeds_at,
    gains_at,
    w_qkv,
    w_out,
    w_up,
    w_down,
    cache,
    lengths_at,
    heads_at,
    blocks_at,
    counts_at,
    out,
    embeds,
    gains,
    lengths,
    heads,
    blocks,
    counts,
    small_sem,
    qkv_w,
    out_w,
    up_w,
    down_w,
    kv,
    load_sem,
    x_in,
    first_in,
    part_out,
    part_in,
    x_recv,
    first_recv,
    part_recv,
    x_send,
    first_send,
    part_send,
    next_send,
    first_own,
    next_own,
):
    segments, members, steps, seqs, micro, groups = sizes
    piece = embeds.shape[1]
    width = piece * members
    rows = steps * seqs // groups
    steps_in = steps // groups
    head_dim = w_qkv.shape[2]
    positions = cache.shape[1] // seqs
    group = seqs // micro
    segment = lax.axis_index("segment")
    rank = lax.axis_index("tensor")
    order = partner_order(members)

    def other(k):
        return lax.rem(rank + k, members)

    small = [
        pltpu.make_async_copy(source, target, small_sem.at[i])
        for i, (source, target) in enumerate(
            [
                (embeds_at, embeds),
                (lengths_at, lengths),
                (heads_at, heads),
                (blocks_at, blocks),
                (counts_at, counts),
                (gains_at, gains),
            ]
        )
    ]
    for load in small:
        load.start()
    loads = [
        pltpu.make_async_copy(
            w_qkv.at[j], qkv_w.at[:, pl.ds(j * head_dim, head_dim)], load_sem.at[j]
        )
        for j in range(3)
    ]
    loads.append(pltpu.make_async_copy(cache, kv, load_sem.at[3]))
    loads.append(pltpu.make_async_copy(w_out, out_w, load_sem.at[4]))
    loads.append(pltpu.make_async_copy(w_up, up_w, load_sem.at[5]))
    loads.append(pltpu.make_async_copy(w_down, down_w, load_sem.at[6]))
    for load in loads:
        load.start()

    barrier = pltpu.get_barrier_semaphore()
    for k in range(1, members):
        pl.semaphore_signal(barrier, inc=1, device_id=(segment, other(k)), device_id_type=MESH_ID)

    @pl.when(segment > 0)
    def _():
        for k in range(members):
            pl.semaphore_signal(
                barrier, inc=1, device_id=(segment - 1, other(k)), device_id_type=MESH_ID
            )

    @pl.when(segment < segments - 1)
    def _():
        for k in range(members):
            pl.semaphore_signal(
                barrier, inc=1, device_id=(segment + 1, other(k)), device_id_type=MESH_ID
            )

    inner = (segment > 0) & (segment < segments - 1)

    @pl.when(inner)
    def _():
        pl.semaphore_wait(barrier, 3 * members - 1)

    @pl.when(jnp.logical_not(inner))
    def _():
        pl.semaphore_wait(barrier, 2 * members - 1)

    def send(src, dst, send_sem, recv_sem, target):
        return pltpu.make_async_remote_copy(
            src_ref=src,
            dst_ref=dst,
            send_sem=send_sem,
            recv_sem=recv_sem,
            device_id=target,
            device_id_type=MESH_ID,
        )

    def arrival(buffer, sem):
        return send(buffer, buffer, sem, sem, (segment, other(1)))

    def x_copy(g, k):
        return send(
            embeds.at[pl.ds(g * rows, rows)],
            x_in.at[g, rank],
            x_send.at[g, k],
            x_recv.at[g, rank],
            (segment, other(k)),
        )

    small[0].wait()

    @pl.when(segment == 0)
    def _():
        for g in range(groups):
            for k in order:
                x_copy(g, k).start()
            x_in[g, rank] = embeds[g * rows : (g + 1) * rows]

    for load in small[1:]:
        load.wait()
    row_ids = lax.broadcasted_iota(jnp.int32, (steps * seqs, 1), 0)
    row_seq = lax.rem(row_ids, seqs)
    row_len = jnp.zeros((steps * seqs, 1), jnp.int32)
    for s in range(seqs):
        row_len = jnp.where(row_seq == s, lengths[s], row_len)

    def live_rows(lists, which):
        live = jnp.zeros((steps * seqs, 1), jnp.int32)
        for t in range(steps):
            for m in range(micro):
                hit = jnp.int32(0)
                for j in range(lists.shape[2]):
                    same = (lists[t, m, j] == rank) & (j < counts[t, m, which])
                    hit = hit + same.astype(jnp.int32)
                start = t * seqs + m * group
                inside = (row_ids >= start) & (row_ids < start + group)
                live = jnp.where(inside, hit, live)
        return live > 0

    head_live = live_rows(heads, 0)
    block_live = live_rows(blocks, 1)

    def span(p):
        return slice(p * piece, (p + 1) * piece)

    def normalized(buffer, g, which):
        total = jnp.zeros((rows, 1), jnp.float32)
        for p in range(members):
            total = total + jnp.sum(buffer[g, p].astype(jnp.float32), -1, keepdims=True)
        mean = total / width
        square = jnp.zeros((rows, 1), jnp.float32)
        for p in range(members):
            off = buffer[g, p].astype(jnp.float32) - mean
            square = square + jnp.sum(off * off, -1, keepdims=True)
        inverse = lax.rsqrt(square / width + EPS)
        for p in range(members):
            off = buffer[g, p].astype(jnp.float32) - mean
            yield p, (off * inverse * gains[which : which + 1, span(p)]).astype(jnp.bfloat16)

    def columns(p):
        return pl.ds(pl.multiple_of(p * piece, piece), piece)

    def part_copy(phase, g, k):
        return send(
            part_out.at[phase, g, k],
            part_in.at[phase, g, rank],
            part_send.at[phase, g, k],
            part_recv.at[phase, g, rank],
            (segment, other(k)),
        )

    def scatter(values, weight, phase, g):
        for k in order:
            part = jnp.dot(values, weight[:, columns(other(k))], preferred_element_type=jnp.float32)
            part_out[phase, g, k] = part.astype(jnp.bfloat16)
            part_copy(phase, g, k).start()
        return jnp.dot(values, weight[:, columns(rank)], preferred_element_type=jnp.float32)

    def gather_sum(total, phase, g):
        for k in order:
            p = other(k)
            arrival(part_in.at[phase, g, p], part_recv.at[phase, g, p]).wait_recv()
            total = total + part_in[phase, g, p].astype(jnp.float32)
        return total

    def first_copy(g, k):
        return send(
            first_own.at[g],
            first_in.at[g, rank],
            first_send.at[g, k],
            first_recv.at[g, rank],
            (segment, other(k)),
        )

    def next_copy(g, k):
        return send(
            next_own.at[g],
            x_in.at[g, rank],
            next_send.at[g, k],
            x_recv.at[g, rank],
            (segment + 1, other(k)),
        )

    fresh_keys, fresh_values = [], []

    def attend(g):
        qkv = jnp.zeros((rows, 3 * head_dim), jnp.float32)
        for p, h in normalized(x_in, g, 0):
            qkv = qkv + jnp.dot(h, qkv_w[span(p), :], preferred_element_type=jnp.float32)
        qkv = qkv.astype(jnp.bfloat16)
        query = qkv[:, :head_dim]
        fresh_keys.append(qkv[:, head_dim : 2 * head_dim])
        fresh_values.append(qkv[:, 2 * head_dim :])
        scale = head_dim ** (-0.5)
        contract = (((1,), (1,)), ((), ()))
        mine = slice(g * rows, (g + 1) * rows)
        old = lax.dot_general(query, kv[0], contract, preferred_element_type=jnp.float32) * scale
        where = lax.broadcasted_iota(jnp.int32, old.shape, 1)
        start = row_seq[mine] * positions
        live = (where >= start) & (where < start + row_len[mine])
        old = jnp.where(live, old, -jnp.inf)
        top = jnp.max(old, -1, keepdims=True)
        fresh = []
        for u, keys in enumerate(fresh_keys):
            new = lax.dot_general(query, keys, contract, preferred_element_type=jnp.float32) * scale
            seen = lax.broadcasted_iota(jnp.int32, new.shape, 1) + u * rows
            seen_ok = (lax.rem(seen, seqs) == row_seq[mine]) & (seen <= row_ids[mine])
            new = jnp.where(seen_ok, new, -jnp.inf)
            top = jnp.maximum(top, jnp.max(new, -1, keepdims=True))
            fresh.append(new)
        old = jnp.exp(old - top)
        norm = jnp.sum(old, -1, keepdims=True)
        fresh = [jnp.exp(new - top) for new in fresh]
        for new in fresh:
            norm = norm + jnp.sum(new, -1, keepdims=True)
        mixed = jnp.dot(
            (old / norm).astype(jnp.bfloat16), kv[1], preferred_element_type=jnp.float32
        )
        for new, values in zip(fresh, fresh_values):
            mixed = mixed + jnp.dot(
                (new / norm).astype(jnp.bfloat16), values, preferred_element_type=jnp.float32
            )
        return jnp.where(head_live[mine], mixed, 0.0).astype(jnp.bfloat16)

    def feed(g):
        upper = jnp.zeros((rows, up_w.shape[1]), jnp.float32)
        for p, h in normalized(first_in, g, 1):
            upper = upper + jnp.dot(h, up_w[span(p), :], preferred_element_type=jnp.float32)
        mine = slice(g * rows, (g + 1) * rows)
        return jnp.where(block_live[mine], jnp.maximum(upper, 0.0), 0.0).astype(jnp.bfloat16)

    sums = [None] * groups
    for g in range(groups):
        for k in order:
            p = other(k)
            arrival(x_in.at[g, p], x_recv.at[g, p]).wait_recv()

        @pl.when(segment > 0)
        def _():
            arrival(x_in.at[g, rank], x_recv.at[g, rank]).wait_recv()

        if g == 0:
            for load in loads[:4]:
                load.wait()
        mixed = attend(g)
        if g == 0:
            loads[4].wait()
        sums[g] = scatter(mixed, out_w, 0, g)
    for g in range(groups):
        attn = gather_sum(sums[g], 0, g)
        first = (x_in[g, rank].astype(jnp.float32) + attn).astype(jnp.bfloat16)
        first_own[g] = first
        for k in order:
            first_copy(g, k).start()
        first_in[g, rank] = first
    for load in loads[5:]:
        load.wait()
    for g in range(groups):
        for k in order:
            p = other(k)
            arrival(first_in.at[g, p], first_recv.at[g, p]).wait_recv()
        sums[g] = scatter(feed(g), down_w, 1, g)
    for g in range(groups):
        lower = gather_sum(sums[g], 1, g)
        result = (first_own[g].astype(jnp.float32) + lower).astype(jnp.bfloat16)
        next_own[g] = result

        @pl.when(segment < segments - 1)
        def _():
            for k in [*order, 0]:
                next_copy(g, k).start()

        out[g * rows : (g + 1) * rows] = result

    for g in range(groups):

        @pl.when(segment == 0)
        def _():
            for k in order:
                x_copy(g, k).wait_send()

        for k in order:
            part_copy(0, g, k).wait_send()
            first_copy(g, k).wait_send()
            part_copy(1, g, k).wait_send()

        @pl.when(segment < segments - 1)
        def _():
            for k in [*order, 0]:
                next_copy(g, k).wait_send()


def body(
    embeds,
    norm_gains,
    w_qkv,
    w_out,
    w_up,
    w_down,
    cache,
    lengths,
    active_heads,
    active_blocks,
    active_counts,
):
    segments = lax.axis_size("segment")
    members = lax.axis_size("tensor")
    steps, seqs, piece = embeds.shape
    micro = active_heads.shape[2]
    width = piece * members
    head_dim = w_qkv.shape[-1]
    block = w_up.shape[2]
    positions = cache.shape[4]
    groups = GROUPS
    rows = steps * seqs // groups
    bf16 = jnp.bfloat16
    vmem = pl.BlockSpec(memory_space=pltpu.VMEM)
    hbm = pl.BlockSpec(memory_space=pl.ANY)
    dma = pltpu.SemaphoreType.DMA
    sizes = (segments, members, steps, seqs, micro, groups)
    flops = 2 * steps * seqs * width * (4 * head_dim + 2 * block)
    states = pl.pallas_call(
        functools.partial(relay_kernel, sizes),
        out_shape=jax.ShapeDtypeStruct((steps * seqs, piece), bf16),
        in_specs=[hbm] * 11,
        out_specs=vmem,
        scratch_shapes=[
            pltpu.VMEM((steps * seqs, piece), bf16),
            pltpu.VMEM(norm_gains.shape[1:], jnp.float32),
            pltpu.SMEM(lengths.shape, jnp.int32),
            pltpu.SMEM(active_heads.shape[1:], jnp.int32),
            pltpu.SMEM(active_blocks.shape[1:], jnp.int32),
            pltpu.SMEM(active_counts.shape[1:], jnp.int32),
            dma((6,)),
            pltpu.VMEM((width, 3 * head_dim), bf16),
            pltpu.VMEM((head_dim, width), bf16),
            pltpu.VMEM((width, block), bf16),
            pltpu.VMEM((block, width), bf16),
            pltpu.VMEM((2, seqs * positions, head_dim), bf16),
            dma((7,)),
            pltpu.VMEM((groups, members, rows, piece), bf16),
            pltpu.VMEM((groups, members, rows, piece), bf16),
            pltpu.VMEM((2, groups, members, rows, piece), bf16),
            pltpu.VMEM((2, groups, members, rows, piece), bf16),
            dma((groups, members)),
            dma((groups, members)),
            dma((2, groups, members)),
            dma((groups, members)),
            dma((groups, members)),
            dma((2, groups, members)),
            dma((groups, members)),
            pltpu.VMEM((groups, rows, piece), bf16),
            pltpu.VMEM((groups, rows, piece), bf16),
        ],
        compiler_params=pltpu.CompilerParams(
            collective_id=0, has_side_effects=True, vmem_limit_bytes=56 * 1024 * 1024
        ),
        cost_estimate=pl.CostEstimate(
            flops=flops, bytes_accessed=2 * width * (4 * head_dim + 2 * block), transcendentals=0
        ),
    )(
        embeds.reshape(steps * seqs, piece),
        norm_gains[0],
        jnp.transpose(w_qkv, (0, 2, 3, 1, 4)).reshape(3, width, head_dim),
        w_out[0, 0],
        w_up[0],
        w_down[0],
        cache.reshape(2, seqs * positions, head_dim),
        lengths,
        active_heads[0],
        active_blocks[0],
        active_counts[0],
    )
    return states.reshape(1, steps, seqs, piece)


def solution(mesh):
    in_specs = (
        P(None, None, "tensor"),
        P("segment", None, None),
        P("segment", None, None, "tensor", None),
        P("segment", "tensor", None, None),
        P("segment", None, "tensor"),
        P("segment", "tensor", None),
        P("segment", None, None, "tensor", None, None),
        P(),
        P("segment", None, None, None),
        P("segment", None, None, None),
        P("segment", None, None, None),
    )
    out_specs = P("segment", None, None, "tensor")
    return jax.shard_map(body, mesh=mesh, in_specs=in_specs, out_specs=out_specs, check_vma=False)
```

```python
import functools

import jax
import jax.numpy as jnp
from jax import lax
from jax.experimental import pallas as pl
from jax.experimental.pallas import tpu as pltpu
from jax.sharding import PartitionSpec as P

EPS = 1e-05
GROUPS = 2
MESH_ID = pl.DeviceIdType.MESH


def partner_order(members):
    return list(range(1, members))


def relay_kernel(
    sizes,
    embeds_at,
    gains_at,
    w_qkv,
    w_out,
    w_up,
    w_down,
    cache,
    lengths_at,
    heads_at,
    blocks_at,
    counts_at,
    out,
    embeds,
    gains,
    lengths,
    heads,
    blocks,
    counts,
    small_sem,
    qkv_w,
    out_w,
    up_w,
    down_w,
    kv,
    load_sem,
    x_in,
    first_in,
    part_out,
    part_in,
    x_recv,
    first_recv,
    part_recv,
    x_send,
    first_send,
    part_send,
    next_send,
    first_own,
    next_own,
):
    segments, members, steps, seqs, micro, groups = sizes
    piece = embeds.shape[1]
    width = piece * members
    rows = steps * seqs // groups
    steps_in = steps // groups
    head_dim = w_qkv.shape[2]
    positions = cache.shape[1] // seqs
    group = seqs // micro
    segment = lax.axis_index("segment")
    rank = lax.axis_index("tensor")
    order = partner_order(members)

    def other(k):
        return lax.rem(rank + k, members)

    small = [
        pltpu.make_async_copy(source, target, small_sem.at[i])
        for i, (source, target) in enumerate(
            [
                (embeds_at, embeds),
                (lengths_at, lengths),
                (heads_at, heads),
                (blocks_at, blocks),
                (counts_at, counts),
                (gains_at, gains),
            ]
        )
    ]
    for load in small:
        load.start()
    loads = [
        pltpu.make_async_copy(
            w_qkv.at[j], qkv_w.at[:, pl.ds(j * head_dim, head_dim)], load_sem.at[j]
        )
        for j in range(3)
    ]
    loads.append(pltpu.make_async_copy(cache, kv, load_sem.at[3]))
    loads.append(pltpu.make_async_copy(w_out, out_w, load_sem.at[4]))
    loads.append(pltpu.make_async_copy(w_up, up_w, load_sem.at[5]))
    loads.append(pltpu.make_async_copy(w_down, down_w, load_sem.at[6]))
    for load in loads:
        load.start()

    barrier = pltpu.get_barrier_semaphore()
    for k in range(1, members):
        pl.semaphore_signal(barrier, inc=1, device_id=(segment, other(k)), device_id_type=MESH_ID)

    @pl.when(segment > 0)
    def _():
        for k in range(members):
            pl.semaphore_signal(
                barrier, inc=1, device_id=(segment - 1, other(k)), device_id_type=MESH_ID
            )

    @pl.when(segment < segments - 1)
    def _():
        for k in range(members):
            pl.semaphore_signal(
                barrier, inc=1, device_id=(segment + 1, other(k)), device_id_type=MESH_ID
            )

    inner = (segment > 0) & (segment < segments - 1)

    @pl.when(inner)
    def _():
        pl.semaphore_wait(barrier, 3 * members - 1)

    @pl.when(jnp.logical_not(inner))
    def _():
        pl.semaphore_wait(barrier, 2 * members - 1)

    def send(src, dst, send_sem, recv_sem, target):
        return pltpu.make_async_remote_copy(
            src_ref=src,
            dst_ref=dst,
            send_sem=send_sem,
            recv_sem=recv_sem,
            device_id=target,
            device_id_type=MESH_ID,
        )

    def arrival(buffer, sem):
        return send(buffer, buffer, sem, sem, (segment, other(1)))

    def x_copy(g, k):
        return send(
            embeds.at[pl.ds(g * rows, rows)],
            x_in.at[g, rank],
            x_send.at[g, k],
            x_recv.at[g, rank],
            (segment, other(k)),
        )

    small[0].wait()

    @pl.when(segment == 0)
    def _():
        for g in range(groups):
            for k in order:
                x_copy(g, k).start()
            x_in[g, rank] = embeds[g * rows : (g + 1) * rows]

    for load in small[1:]:
        load.wait()
    row_ids = lax.broadcasted_iota(jnp.int32, (steps * seqs, 1), 0)
    row_seq = lax.rem(row_ids, seqs)
    row_len = jnp.zeros((steps * seqs, 1), jnp.int32)
    for s in range(seqs):
        row_len = jnp.where(row_seq == s, lengths[s], row_len)

    def live_rows(lists, which):
        live = jnp.zeros((steps * seqs, 1), jnp.int32)
        for t in range(steps):
            for m in range(micro):
                hit = jnp.int32(0)
                for j in range(lists.shape[2]):
                    same = (lists[t, m, j] == rank) & (j < counts[t, m, which])
                    hit = hit + same.astype(jnp.int32)
                start = t * seqs + m * group
                inside = (row_ids >= start) & (row_ids < start + group)
                live = jnp.where(inside, hit, live)
        return live > 0

    head_live = live_rows(heads, 0)
    block_live = live_rows(blocks, 1)

    def span(p):
        return slice(p * piece, (p + 1) * piece)

    def normalized(buffer, g, which):
        total = jnp.zeros((rows, 1), jnp.float32)
        for p in range(members):
            total = total + jnp.sum(buffer[g, p].astype(jnp.float32), -1, keepdims=True)
        mean = total / width
        square = jnp.zeros((rows, 1), jnp.float32)
        for p in range(members):
            off = buffer[g, p].astype(jnp.float32) - mean
            square = square + jnp.sum(off * off, -1, keepdims=True)
        inverse = lax.rsqrt(square / width + EPS)
        for p in range(members):
            off = buffer[g, p].astype(jnp.float32) - mean
            yield p, (off * inverse * gains[which : which + 1, span(p)]).astype(jnp.bfloat16)

    def columns(p):
        return pl.ds(pl.multiple_of(p * piece, piece), piece)

    def part_copy(phase, g, k):
        return send(
            part_out.at[phase, g, k],
            part_in.at[phase, g, rank],
            part_send.at[phase, g, k],
            part_recv.at[phase, g, rank],
            (segment, other(k)),
        )

    def scatter(values, weight, phase, g):
        for first in range(0, len(order), (members // 2)):
            batch = order[first : first + (members // 2)]
            for k in batch:
                part = jnp.dot(
                    values, weight[:, columns(other(k))], preferred_element_type=jnp.float32
                )
                part_out[phase, g, k] = part.astype(jnp.bfloat16)
            for k in batch:
                part_copy(phase, g, k).start()
        return jnp.dot(values, weight[:, columns(rank)], preferred_element_type=jnp.float32)

    def gather_sum(total, phase, g):
        for k in order:
            p = other(k)
            arrival(part_in.at[phase, g, p], part_recv.at[phase, g, p]).wait_recv()
        for k in order:
            total = total + part_in[phase, g, other(k)].astype(jnp.float32)
        return total

    def first_copy(g, k):
        return send(
            first_own.at[g],
            first_in.at[g, rank],
            first_send.at[g, k],
            first_recv.at[g, rank],
            (segment, other(k)),
        )

    def next_copy(g, k):
        return send(
            next_own.at[g],
            x_in.at[g, rank],
            next_send.at[g, k],
            x_recv.at[g, rank],
            (segment + 1, other(k)),
        )

    fresh_keys, fresh_values = [], []

    def attend(g):
        qkv = jnp.zeros((rows, 3 * head_dim), jnp.float32)
        for p, h in normalized(x_in, g, 0):
            qkv = qkv + jnp.dot(h, qkv_w[span(p), :], preferred_element_type=jnp.float32)
        qkv = qkv.astype(jnp.bfloat16)
        query = qkv[:, :head_dim]
        fresh_keys.append(qkv[:, head_dim : 2 * head_dim])
        fresh_values.append(qkv[:, 2 * head_dim :])
        scale = head_dim ** (-0.5)
        contract = (((1,), (1,)), ((), ()))
        mine = slice(g * rows, (g + 1) * rows)
        old = lax.dot_general(query, kv[0], contract, preferred_element_type=jnp.float32) * scale
        where = lax.broadcasted_iota(jnp.int32, old.shape, 1)
        start = row_seq[mine] * positions
        live = (where >= start) & (where < start + row_len[mine])
        old = jnp.where(live, old, -jnp.inf)
        top = jnp.max(old, -1, keepdims=True)
        fresh = []
        for u, keys in enumerate(fresh_keys):
            new = lax.dot_general(query, keys, contract, preferred_element_type=jnp.float32) * scale
            seen = lax.broadcasted_iota(jnp.int32, new.shape, 1) + u * rows
            seen_ok = (lax.rem(seen, seqs) == row_seq[mine]) & (seen <= row_ids[mine])
            new = jnp.where(seen_ok, new, -jnp.inf)
            top = jnp.maximum(top, jnp.max(new, -1, keepdims=True))
            fresh.append(new)
        old = jnp.exp(old - top)
        norm = jnp.sum(old, -1, keepdims=True)
        fresh = [jnp.exp(new - top) for new in fresh]
        for new in fresh:
            norm = norm + jnp.sum(new, -1, keepdims=True)
        mixed = jnp.dot(
            (old / norm).astype(jnp.bfloat16), kv[1], preferred_element_type=jnp.float32
        )
        for new, values in zip(fresh, fresh_values):
            mixed = mixed + jnp.dot(
                (new / norm).astype(jnp.bfloat16), values, preferred_element_type=jnp.float32
            )
        return jnp.where(head_live[mine], mixed, 0.0).astype(jnp.bfloat16)

    def feed(g):
        upper = jnp.zeros((rows, up_w.shape[1]), jnp.float32)
        for p, h in normalized(first_in, g, 1):
            upper = upper + jnp.dot(h, up_w[span(p), :], preferred_element_type=jnp.float32)
        mine = slice(g * rows, (g + 1) * rows)
        return jnp.where(block_live[mine], jnp.maximum(upper, 0.0), 0.0).astype(jnp.bfloat16)

    sums = [None] * groups
    for g in range(groups):
        for k in order:
            p = other(k)
            arrival(x_in.at[g, p], x_recv.at[g, p]).wait_recv()

        @pl.when(segment > 0)
        def _():
            arrival(x_in.at[g, rank], x_recv.at[g, rank]).wait_recv()

        if g == 0:
            for load in loads[:4]:
                load.wait()
        mixed = attend(g)
        if g == 0:
            loads[4].wait()
        sums[g] = scatter(mixed, out_w, 0, g)
    for g in range(groups):
        attn = gather_sum(sums[g], 0, g)
        first = (x_in[g, rank].astype(jnp.float32) + attn).astype(jnp.bfloat16)
        first_own[g] = first
        for k in order:
            first_copy(g, k).start()
        first_in[g, rank] = first
    for load in loads[5:]:
        load.wait()
    for g in range(groups):
        for k in order:
            p = other(k)
            arrival(first_in.at[g, p], first_recv.at[g, p]).wait_recv()
        sums[g] = scatter(feed(g), down_w, 1, g)
    for g in range(groups):
        lower = gather_sum(sums[g], 1, g)
        result = (first_own[g].astype(jnp.float32) + lower).astype(jnp.bfloat16)
        next_own[g] = result

        @pl.when(segment < segments - 1)
        def _():
            for k in [*order, 0]:
                next_copy(g, k).start()

        out[g * rows : (g + 1) * rows] = result

    for g in range(groups):

        @pl.when(segment == 0)
        def _():
            for k in order:
                x_copy(g, k).wait_send()

        for k in order:
            part_copy(0, g, k).wait_send()
            first_copy(g, k).wait_send()
            part_copy(1, g, k).wait_send()

        @pl.when(segment < segments - 1)
        def _():
            for k in [*order, 0]:
                next_copy(g, k).wait_send()


def body(
    embeds,
    norm_gains,
    w_qkv,
    w_out,
    w_up,
    w_down,
    cache,
    lengths,
    active_heads,
    active_blocks,
    active_counts,
):
    segments = lax.axis_size("segment")
    members = lax.axis_size("tensor")
    steps, seqs, piece = embeds.shape
    micro = active_heads.shape[2]
    width = piece * members
    head_dim = w_qkv.shape[-1]
    block = w_up.shape[2]
    positions = cache.shape[4]
    groups = GROUPS
    rows = steps * seqs // groups
    bf16 = jnp.bfloat16
    vmem = pl.BlockSpec(memory_space=pltpu.VMEM)
    hbm = pl.BlockSpec(memory_space=pl.ANY)
    dma = pltpu.SemaphoreType.DMA
    sizes = (segments, members, steps, seqs, micro, groups)
    flops = 2 * steps * seqs * width * (4 * head_dim + 2 * block)
    states = pl.pallas_call(
        functools.partial(relay_kernel, sizes),
        out_shape=jax.ShapeDtypeStruct((steps * seqs, piece), bf16),
        in_specs=[hbm] * 11,
        out_specs=vmem,
        scratch_shapes=[
            pltpu.VMEM((steps * seqs, piece), bf16),
            pltpu.VMEM(norm_gains.shape[1:], jnp.float32),
            pltpu.SMEM(lengths.shape, jnp.int32),
            pltpu.SMEM(active_heads.shape[1:], jnp.int32),
            pltpu.SMEM(active_blocks.shape[1:], jnp.int32),
            pltpu.SMEM(active_counts.shape[1:], jnp.int32),
            dma((6,)),
            pltpu.VMEM((width, 3 * head_dim), bf16),
            pltpu.VMEM((head_dim, width), bf16),
            pltpu.VMEM((width, block), bf16),
            pltpu.VMEM((block, width), bf16),
            pltpu.VMEM((2, seqs * positions, head_dim), bf16),
            dma((7,)),
            pltpu.VMEM((groups, members, rows, piece), bf16),
            pltpu.VMEM((groups, members, rows, piece), bf16),
            pltpu.VMEM((2, groups, members, rows, piece), bf16),
            pltpu.VMEM((2, groups, members, rows, piece), bf16),
            dma((groups, members)),
            dma((groups, members)),
            dma((2, groups, members)),
            dma((groups, members)),
            dma((groups, members)),
            dma((2, groups, members)),
            dma((groups, members)),
            pltpu.VMEM((groups, rows, piece), bf16),
            pltpu.VMEM((groups, rows, piece), bf16),
        ],
        compiler_params=pltpu.CompilerParams(
            collective_id=0, has_side_effects=True, vmem_limit_bytes=56 * 1024 * 1024
        ),
        cost_estimate=pl.CostEstimate(
            flops=flops, bytes_accessed=2 * width * (4 * head_dim + 2 * block), transcendentals=0
        ),
    )(
        embeds.reshape(steps * seqs, piece),
        norm_gains[0],
        jnp.transpose(w_qkv, (0, 2, 3, 1, 4)).reshape(3, width, head_dim),
        w_out[0, 0],
        w_up[0],
        w_down[0],
        cache.reshape(2, seqs * positions, head_dim),
        lengths,
        active_heads[0],
        active_blocks[0],
        active_counts[0],
    )
    return states.reshape(1, steps, seqs, piece)


def solution(mesh):
    in_specs = (
        P(None, None, "tensor"),
        P("segment", None, None),
        P("segment", None, None, "tensor", None),
        P("segment", "tensor", None, None),
        P("segment", None, "tensor"),
        P("segment", "tensor", None),
        P("segment", None, None, "tensor", None, None),
        P(),
        P("segment", None, None, None),
        P("segment", None, None, None),
        P("segment", None, None, None),
    )
    out_specs = P("segment", None, None, "tensor")
    return jax.shard_map(body, mesh=mesh, in_specs=in_specs, out_specs=out_specs, check_vma=False)
```
